256 devices in a mesh: table: 64 (over y, z, core), helper: 4 (over x).
Axes of the slice: x: 4, y: 4, z: 8, core: 2. Of those that a mesh axis runs over, the one named last changes fastest.
Arguments:
- tables: bfloat16 [512, 4096, 128], P('table'), may hold values from -6 to 6
- projections: bfloat16 [512, 128, 256], P('table'), may hold values from -0.0078125 to 0.0078125
- bag_rows: int32 [512, 64, 4, 8, 16], P('table', None, 'helper'), may hold values from 0 to 4095
- bag_lengths: int32 [512, 64, 4, 8], P('table', None, 'helper'), may hold values from 1 to 16
- candidates: bfloat16 [64, 4, 2048, 256], P('table', 'helper'), may hold values from -6 to 6
- request_counts: int32 [64, 4, 8], P('table', 'helper'), may hold values from 1 to 1024, as said below
- cross_down: bfloat16 [3, 512, 128], replicated, may hold values from -0.25 to 0.25
- cross_up: bfloat16 [3, 128, 512], replicated, may hold values from -0.5 to 0.5
- cross_bias: float32 [3, 512], replicated, may hold values from -3 to 3
- layer_one: bfloat16 [512, 1024], replicated, may hold values from -0.25 to 0.25
- bias_one: float32 [1024], replicated, may hold values from -2 to 2
- layer_two: bfloat16 [1024, 512], replicated, may hold values from -0.1875 to 0.1875
- bias_two: float32 [512], replicated, may hold values from -2 to 2
- layer_three: bfloat16 [512, 256], replicated, may hold values from -0.25 to 0.25
- bias_three: float32 [256], replicated, may hold values from -2 to 2
- score_weight: bfloat16 [256], replicated, may hold values from -0.375 to 0.375
Outputs:
- scores: float32 [64, 4, 2048], P('table', 'helper')
The draws below stay inside these ranges and needn't reach their ends.
Inputs may be any that keep to these rules, and one draw needn't show every extreme that they name: For each (a, h) the 8 counts request_counts[a, h, :] sum to at most 2048; for every a exactly one h has a sum of exactly 2048, and in that list the first request holds exactly 1024 candidates.
All inputs are finite; a program needn't handle non-finite values.
Results may differ from the reference program's by a relative error of at most 0.018.
Values may be sent and summed in bfloat16 or wider, within the bound.
No kernel may reach another device: no remote copies, remote signals or barrier semaphores. Data moves between devices by JAX's collectives and lax.ppermute only.
A program may use at most 128 MiB of HBM per device.

```python
import math
import jax
import jax.numpy as jnp
import numpy as np
from jax import lax

E = 128
P_SIZE = 256
RANK = 128
H1 = 1024
H2 = 512
H3 = 256
ROWS = 4096
CROSS = 3
BLOCK = 256
BAG = 16
REQ_DEV = 8
BLK_DEV = 8
NTAB = 512
SLOTS = 2048
D0 = 512
N_TABLE = 64
N_HELPER = 4


def split_total(key, totals, parts):
    shares = jax.random.randint(key, totals.shape + (parts,), 1, 5)
    running = jnp.cumsum(shares, axis=-1)
    ends = totals[..., None] * running // running[..., -1:]
    starts = jnp.concatenate([jnp.zeros_like(ends[..., :1]), ends[..., :-1]], axis=-1)
    return (ends - starts).astype(jnp.int32)


def draw_request_counts(key, part):
    first, second, third, fourth = jax.random.split(jax.random.fold_in(key, 11), 4)
    lowest = max(BLOCK // 2, 4 * REQ_DEV)
    highest = SLOTS // 2
    totals = jax.random.randint(first, (N_TABLE, N_HELPER), lowest, highest + 1)
    fullest = jax.random.randint(second, (N_TABLE,), 0, N_HELPER)
    helpers = jnp.arange(N_HELPER, dtype=jnp.int32)
    is_full = helpers[None, :] == fullest[:, None]
    drawn = split_total(third, totals, REQ_DEV)
    if REQ_DEV == 1:
        full_counts = jnp.full((N_TABLE, N_HELPER, 1), SLOTS, jnp.int32)
    else:
        leading = SLOTS // 2
        rest = split_total(fourth, jnp.full((N_TABLE, N_HELPER), SLOTS - leading, jnp.int32), REQ_DEV - 1)
        full_counts = jnp.concatenate([jnp.full((N_TABLE, N_HELPER, 1), leading, jnp.int32), rest], axis=-1)
    return jnp.where(is_full[..., None], full_counts, drawn).astype(jnp.int32)


def touch_ends(values, stream_key, low, largest):
    longest = values.shape.index(max(values.shape))
    spots = []
    for shift in (0, 1):
        where = [jax.random.randint(jax.random.fold_in(stream_key, axis), (), 0, length) for axis, length in enumerate(values.shape)]
        where[longest] = (where[longest] + shift) % values.shape[longest]
        spots.append(tuple(where))
    return values.at[spots[0]].set(low).at[spots[1]].set(largest)


def level_of(rng, extent, cuts, least, high):
    def one(dim, shards_of):
        draws = jax.random.uniform(jax.random.fold_in(jax.random.fold_in(rng, 6), dim), (shards_of,), jnp.float32, least / len(cuts), high / len(cuts))
        return jnp.repeat(jnp.exp(draws), extent[dim] // shards_of).reshape((-1,) + (1,) * (len(extent) - dim - 1))

    factor_of = one(*cuts[0])
    for cut in cuts[1:]:
        factor_of = factor_of * one(*cut)
    return factor_of


def cumulative_ranks(amount, slope):
    portions = [(1 << 20) // math.isqrt(standing ** slope) + 1 for standing in range(1, amount + 1)]
    spread = 1 + sum(portions) // (1 << 30)
    return np.cumsum(np.array([max(1, weight // spread) for weight in portions]))


def ranked(stream_key, extent, number_of, lean):
    table = cumulative_ranks(number_of, lean)
    lot = jax.random.randint(jax.random.fold_in(stream_key, 1), extent, 0, int(table[number_of - 1]))
    rank = jnp.searchsorted(jnp.asarray(table, jnp.int32), lot, side="right")
    return jax.random.permutation(jax.random.fold_in(stream_key, 2), number_of)[rank].astype(jnp.int32)


def scatter_about(stream_key, dims, spread, limit, cuts=(), kind=jnp.bfloat16):
    entries = jax.random.normal(stream_key, dims, jnp.float32) * spread
    if len(cuts) > 0:
        entries = level_of(stream_key, dims, cuts, -0.22, 0.18) * entries
    return jnp.clip(entries, min=-limit, max=limit).astype(kind)


def setup_inputs(seed: int = 0) -> dict:
    arg_keys = jax.random.split(jax.random.key(seed), 17)
    tables = scatter_about(arg_keys[0], (NTAB, ROWS, E), 1.0, 6.0, ((0, 64),))
    projections = scatter_about(arg_keys[1], (NTAB, E, P_SIZE), (E * BAG * NTAB // 2) ** -0.5, 0.0078125, ((0, 64),))
    bag_rows = touch_ends(ranked(arg_keys[2], (NTAB, N_TABLE, N_HELPER, REQ_DEV, BAG), ROWS, 2), jax.random.fold_in(arg_keys[2], 3), 0, ROWS - 1).astype(jnp.int32)
    bag_lengths = touch_ends(jax.random.randint(arg_keys[3], (NTAB, N_TABLE, N_HELPER, REQ_DEV), 1, BAG + 1), jax.random.fold_in(arg_keys[3], 1), 1, BAG).astype(jnp.int32)
    candidates = scatter_about(arg_keys[4], (N_TABLE, N_HELPER, SLOTS, P_SIZE), 1.0, 6.0, ((0, 64), (1, 4)))
    request_counts = draw_request_counts(jax.random.fold_in(arg_keys[16], 71), 0)
    cross_down = scatter_about(arg_keys[6], (CROSS, D0, RANK), D0 ** -0.5, 0.25)
    cross_up = scatter_about(arg_keys[7], (CROSS, RANK, D0), RANK ** -0.5, 0.5)
    cross_bias = scatter_about(arg_keys[8], (CROSS, D0), 0.5, 3.0, (), jnp.float32)
    layer_one = scatter_about(arg_keys[9], (D0, H1), D0 ** -0.5, 0.25)
    bias_one = scatter_about(arg_keys[10], (H1,), 0.3, 2.0, (), jnp.float32)
    layer_two = scatter_about(arg_keys[11], (H1, H2), H1 ** -0.5, 0.1875)
    bias_two = scatter_about(arg_keys[12], (H2,), 0.3, 2.0, (), jnp.float32)
    layer_three = scatter_about(arg_keys[13], (H2, H3), H2 ** -0.5, 0.25)
    bias_three = scatter_about(arg_keys[14], (H3,), 0.3, 2.0, (), jnp.float32)
    score_weight = scatter_about(arg_keys[15], (H3,), H3 ** -0.5, 0.375)
    return {"tables": tables, "projections": projections, "bag_rows": bag_rows, "bag_lengths": bag_lengths, "candidates": candidates, "request_counts": request_counts, "cross_down": cross_down, "cross_up": cross_up, "cross_bias": cross_bias, "layer_one": layer_one, "bias_one": bias_one, "layer_two": layer_two, "bias_two": bias_two, "layer_three": layer_three, "bias_three": bias_three, "score_weight": score_weight}


def cross_network(features, context_rows, live_slots, weights):
    cross_down, cross_up, cross_bias, layer_one, bias_one, layer_two, bias_two, layer_three, bias_three, score_weight = weights
    cross_input = jnp.concatenate([features, context_rows], axis=1)
    anchor = cross_input.astype(jnp.float32)
    current = anchor
    for layer_number in range(cross_down.shape[0]):
        reduced = jnp.dot(current.astype(jnp.bfloat16), cross_down[layer_number], preferred_element_type=jnp.float32).astype(jnp.bfloat16)
        current = anchor * (jnp.dot(reduced, cross_up[layer_number], preferred_element_type=jnp.float32) + cross_bias[layer_number]) + current
    hidden = jax.nn.relu(jnp.dot(current.astype(jnp.bfloat16), layer_one, preferred_element_type=jnp.float32) + bias_one).astype(jnp.bfloat16)
    hidden = jax.nn.relu(jnp.dot(hidden, layer_two, preferred_element_type=jnp.float32) + bias_two).astype(jnp.bfloat16)
    hidden = jax.nn.relu(jnp.dot(hidden, layer_three, preferred_element_type=jnp.float32) + bias_three).astype(jnp.bfloat16)
    result = jnp.dot(hidden, score_weight, preferred_element_type=jnp.float32)
    return jnp.where(live_slots, result, jnp.zeros_like(result))


def block_scores(features, codes, context, weights):
    labels = jnp.arange(context.shape[0], dtype=jnp.int32)
    choose = (codes[:, None] == labels[None, :]).astype(jnp.bfloat16)
    context_rows = jnp.dot(choose, context, preferred_element_type=jnp.float32).astype(jnp.bfloat16)
    return cross_network(features, context_rows, codes >= 0, weights)


def slot_codes(counts, total_slots):
    ends = jnp.cumsum(counts)
    positions = jnp.arange(total_slots, dtype=jnp.int32)
    owner = jnp.sum((positions[:, None] >= ends[None, :]).astype(jnp.int32), axis=1)
    return jnp.where(owner < counts.shape[0], owner, -1).astype(jnp.int32)


def reference(tables, projections, bag_rows, bag_lengths, candidates, request_counts, cross_down, cross_up, cross_bias, layer_one, bias_one, layer_two, bias_two, layer_three, bias_three, score_weight):
    weights = (cross_down, cross_up, cross_bias, layer_one, bias_one, layer_two, bias_two, layer_three, bias_three, score_weight)

    def add_table(total, pieces):
        table, projection, indices, lengths = pieces
        looked = table[indices]
        keep = jnp.arange(indices.shape[-1], dtype=jnp.int32) < lengths[..., None]
        pooled = jnp.sum(jnp.where(keep[..., None], looked, jnp.zeros_like(looked)), axis=-2, dtype=jnp.float32).astype(jnp.bfloat16)
        projected = jnp.dot(pooled.reshape(-1, pooled.shape[-1]), projection, preferred_element_type=jnp.float32).astype(jnp.bfloat16)
        projected = lax.optimization_barrier(projected)
        return total + projected.astype(jnp.float32).reshape(total.shape), None

    start = jnp.zeros((N_TABLE, N_HELPER, REQ_DEV, P_SIZE), jnp.float32)
    total, ignored = lax.scan(add_table, start, (tables, projections, bag_rows, bag_lengths))
    context = total.astype(jnp.bfloat16)
    codes = jax.vmap(jax.vmap(lambda counts: slot_codes(counts, SLOTS)))(request_counts)
    count_blocks = N_TABLE * N_HELPER * BLK_DEV
    feature_blocks = candidates.reshape(count_blocks, BLOCK, P_SIZE)
    code_blocks = codes.reshape(count_blocks, BLOCK)
    context_blocks = jnp.repeat(context.reshape(N_TABLE * N_HELPER, REQ_DEV, P_SIZE), BLK_DEV, axis=0)

    def one_block(pieces):
        features, block_codes, block_context = pieces
        return lax.cond(block_codes[0] >= 0,
                        lambda: block_scores(features, block_codes, block_context, weights),
                        lambda: jnp.zeros((BLOCK,), jnp.float32))

    scores = lax.map(one_block, (feature_blocks, code_blocks, context_blocks))
    return scores.reshape(N_TABLE, N_HELPER, SLOTS)
```

```python
import functools

import jax
import jax.numpy as jnp
from jax import lax
from jax.experimental import pallas as pl
from jax.experimental.pallas import tpu as pltpu
from jax.sharding import PartitionSpec as P

HI = 16
LO = 256


def pool_kernel(rows_ref, lens_ref, table_ref, proj_ref, out_ref, hi_ref, lo_ref, tally_ref, total_ref, *, unroll, nt):
    step = pl.program_id(0)
    owners = rows_ref.shape[2]
    span = rows_ref.shape[1]
    requests = lens_ref.shape[1]
    bag = span // requests
    rows = rows_ref[0]
    place = lax.broadcasted_iota(jnp.int32, (requests, bag, owners), 1)
    used = (place < lens_ref[0][:, None, :]).reshape(span, owners)
    high = jnp.where(used, rows // LO, 4 * HI).astype(jnp.float32)
    low = (rows % LO).astype(jnp.float32)
    hi_ref[...] = high.T
    if nt:
        lo_ref[...] = low.T
    else:
        lo_ref[...] = low
    sub = lax.broadcasted_iota(jnp.int32, (requests, span), 0)
    lane = lax.broadcasted_iota(jnp.int32, (requests, span), 1)
    own = lane // bag == sub
    one = jnp.ones((), jnp.bfloat16)
    zero = jnp.zeros((), jnp.bfloat16)
    if nt:
        lo_iota = lax.broadcasted_iota(jnp.int32, (LO, span), 0).astype(jnp.float32).astype(jnp.bfloat16)
    else:
        lo_iota = lax.broadcasted_iota(jnp.int32, (span, LO), 1).astype(jnp.float32).astype(jnp.bfloat16)

    def one_owner(o):
        row = jnp.broadcast_to(hi_ref[pl.ds(o, 1), :], (requests, span))
        code = jnp.where(own, row, 4.0 * HI)
        pair = jnp.concatenate([code, code - 1.0], axis=0).astype(jnp.bfloat16)
        lhs = jnp.concatenate([jnp.where(pair == jnp.bfloat16(2 * k), one, zero) for k in range(HI // 2)], axis=0)
        if nt:
            col = jnp.broadcast_to(lo_ref[pl.ds(o, 1), :], (16, span)).astype(jnp.bfloat16)
            col = jnp.concatenate([col] * (LO // 16), axis=0)
            rhs = jnp.where(col == lo_iota, one, zero)
            return lax.dot_general(lhs, rhs, (((1,), (1,)), ((), ())), preferred_element_type=jnp.float32)
        col = jnp.broadcast_to(lo_ref[:, o : o + 1].astype(jnp.bfloat16), (span, LO))
        rhs = jnp.where(col == lo_iota, one, zero)
        return jnp.dot(lhs, rhs, preferred_element_type=jnp.float32)

    def pairs(p, carry):
        for u in range(unroll):
            q = p * unroll + u
            a = one_owner(2 * q)
            b = one_owner(2 * q + 1)
            at = q * 16 if isinstance(q, int) else pl.multiple_of(q * 16, 16)
            for k in range(HI):
                both = jnp.concatenate([a[k * 8 : k * 8 + 8], b[k * 8 : k * 8 + 8]], axis=0)
                tally_ref[pl.ds(at, 16), k * LO : (k + 1) * LO] = both.astype(jnp.bfloat16)
        return carry

    n = owners // 2 // unroll
    if n == 1 or not nt:
        for p in range(n):
            pairs(p, 0)
    else:
        lax.fori_loop(0, n, pairs, 0)
    pooled = jnp.dot(tally_ref[...], table_ref[0], preferred_element_type=jnp.float32).astype(jnp.bfloat16)
    part = jnp.dot(pooled, proj_ref[0], preferred_element_type=jnp.float32)

    @pl.when(step == 0)
    def _():
        total_ref[...] = part

    @pl.when(step > 0)
    def _():
        total_ref[...] += part

    @pl.when(step == pl.num_programs(0) - 1)
    def _():
        out_ref[...] = total_ref[...].astype(jnp.bfloat16)


def pool(tables, projections, bag_rows, bag_lengths, unroll=32, nt=False):
    nt_, rows, e = tables.shape
    owners, requests, bag = bag_rows.shape[1], bag_rows.shape[3], bag_rows.shape[4]
    width = projections.shape[2]
    r = bag_rows.transpose(0, 2, 3, 4, 1).reshape(nt_, requests * bag, owners)
    l = bag_lengths.transpose(0, 2, 3, 1).reshape(nt_, requests, owners)
    bags = owners * requests
    span = requests * bag
    return pl.pallas_call(
        functools.partial(pool_kernel, unroll=unroll, nt=nt),
        grid=(nt_,),
        in_specs=[
            pl.BlockSpec((1, span, owners), lambda i: (i, 0, 0)),
            pl.BlockSpec((1, requests, owners), lambda i: (i, 0, 0)),
            pl.BlockSpec((1, rows, e), lambda i: (i, 0, 0)),
            pl.BlockSpec((1, e, width), lambda i: (i, 0, 0)),
        ],
        out_specs=pl.BlockSpec((bags, width), lambda i: (0, 0)),
        out_shape=jax.ShapeDtypeStruct((bags, width), jnp.bfloat16),
        scratch_shapes=[
            pltpu.VMEM((owners, span), jnp.float32),
            pltpu.VMEM((owners, span) if nt else (span, owners), jnp.float32),
            pltpu.VMEM((bags, rows), jnp.bfloat16),
            pltpu.VMEM((bags, width), jnp.float32),
        ],
        compiler_params=pltpu.CompilerParams(vmem_limit_bytes=54 << 20),
        name="pool",
    )(r, l, tables, projections)


F32 = jnp.float32
BF = jnp.bfloat16


def score_kernel(counts_ref, got_ref, feat_ref, down_ref, up_ref, cb_ref, w1, b1, w2, b2, w3, b3, ws, out_ref, ctx_ref, *, sub):
    step = pl.program_id(0)
    block = feat_ref.shape[0]
    requests = counts_ref.shape[0]

    @pl.when(step == 0)
    def _():
        got = got_ref[...].astype(F32)
        ctx_ref[...] = jnp.sum(got.reshape(-1, requests, got.shape[1]), axis=0).astype(BF)

    ends = []
    total = jnp.int32(0)
    for r in range(requests):
        total = total + counts_ref[r]
        ends.append(total)
    base = step * block

    @pl.when(base >= total)
    def _():
        out_ref[...] = jnp.zeros_like(out_ref)

    @pl.when(base < total)
    def _():
        lane = lax.broadcasted_iota(jnp.int32, (1, requests), 1)
        end_row = jnp.zeros((1, requests), jnp.int32)
        start_row = jnp.zeros((1, requests), jnp.int32)
        for r in range(requests):
            end_row = jnp.where(lane == r, ends[r], end_row)
            if r:
                start_row = jnp.where(lane == r, ends[r - 1], start_row)
        xs, anchors = [], []
        n = block // sub
        for i in range(n):
            pos = base + i * sub + lax.broadcasted_iota(jnp.int32, (sub, requests), 0)
            choose = ((pos >= start_row) & (pos < end_row)).astype(F32).astype(BF)
            rows = jnp.dot(choose, ctx_ref[...], preferred_element_type=F32)
            a = jnp.concatenate([feat_ref[i * sub : (i + 1) * sub, :].astype(F32), rows], axis=1)
            anchors.append(a)
            xs.append(a)
        for l in range(down_ref.shape[0]):
            red = [jnp.dot(x.astype(BF), down_ref[l], preferred_element_type=F32).astype(BF) for x in xs]
            xs = [
                a * (jnp.dot(r, up_ref[l], preferred_element_type=F32) + cb_ref[l : l + 1, :]) + x
                for a, r, x in zip(anchors, red, xs)
            ]
        hs = [x.astype(BF) for x in xs]
        for w, b in ((w1, b1), (w2, b2), (w3, b3)):
            hs = [jnp.maximum(jnp.dot(h, w[...], preferred_element_type=F32) + b[...], 0.0).astype(BF) for h in hs]
        for i, h in enumerate(hs):
            s = lax.dot_general(ws[...], h, (((1,), (1,)), ((), ())), preferred_element_type=F32)
            at = base + i * sub + lax.broadcasted_iota(jnp.int32, (1, sub), 1)
            out_ref[:, i * sub : (i + 1) * sub] = jnp.where(at < total, s, 0.0)


def score(got, counts, features, cross_down, cross_up, cross_bias, w1, b1, w2, b2, w3, b3, ws, block=1024, sub=512):
    slots, width = features.shape
    requests = counts.shape[0]
    whole = lambda a: pl.BlockSpec(a.shape, lambda i, c: (0,) * a.ndim)
    rest = (cross_down, cross_up, cross_bias, w1, b1[None], w2, b2[None], w3, b3[None], ws[None])
    out = pl.pallas_call(
        functools.partial(score_kernel, sub=sub),
        grid_spec=pltpu.PrefetchScalarGridSpec(
            num_scalar_prefetch=1,
            grid=(slots // block,),
            in_specs=[whole(got), pl.BlockSpec((block, width), lambda i, c: (i, 0))] + [whole(a) for a in rest],
            out_specs=pl.BlockSpec((1, block), lambda i, c: (0, i)),
            scratch_shapes=[pltpu.VMEM((requests, width), BF)],
        ),
        out_shape=jax.ShapeDtypeStruct((1, slots), F32),
        compiler_params=pltpu.CompilerParams(vmem_limit_bytes=40 << 20),
        name="score",
    )(counts, got, features, *rest)
    return out


def body(tables, projections, bag_rows, bag_lengths, candidates, request_counts, *weights):
    owners, requests, width = bag_rows.shape[1], bag_rows.shape[3], projections.shape[2]
    sums = pool(tables, projections, bag_rows, bag_lengths)
    sums = sums.reshape(owners, requests, width)
    got = lax.all_to_all(sums, "table", split_axis=0, concat_axis=0, tiled=True)
    scores = score(got.reshape(owners * requests, width), request_counts[0, 0], candidates[0, 0], *weights)
    return scores[None]


def solution(mesh):
    in_specs = (
        P("table", None, None),
        P("table", None, None),
        P("table", None, "helper", None, None),
        P("table", None, "helper", None),
        P("table", "helper", None, None),
        P("table", "helper", None),
    ) + (P(),) * 10
    out_specs = P("table", "helper", None)
    return jax.shard_map(body, mesh=mesh, in_specs=in_specs, out_specs=out_specs, check_vma=False)
```

```python
import functools

import jax
import jax.numpy as jnp
from jax import lax
from jax.experimental import pallas as pl
from jax.experimental.pallas import tpu as pltpu
from jax.sharding import PartitionSpec as P

F32 = jnp.float32
BF = jnp.bfloat16
HI = 16
LO = 256
F8 = jnp.float8_e4m3fn
UP = 64.0
FINE = 16.0


def pool_kernel(
    rows_ref, lens_ref, table_ref, proj_ref, b1_ref, b2_ref, b3_ref, cb_ref, ws_ref,
    mine_ref, twin_ref, small_ref, hi_ref, lo_ref, tally_a, tally_b, tab_a, tab_b, acc_ref, total_ref, *, chunks, nt, axis
):
    step = pl.program_id(0)
    last = pl.num_programs(0) - 1
    owners = rows_ref.shape[2]
    span = rows_ref.shape[1]
    requests = lens_ref.shape[1]
    bag = span // requests
    total_rows = table_ref.shape[1]

    def prepare():
        rows = rows_ref[0]
        place = lax.broadcasted_iota(jnp.int32, (requests, bag, owners), 1)
        used = (place < lens_ref[0][:, None, :]).reshape(span, owners)
        hi_ref[...] = jnp.where(used, rows // LO, 4 * HI).astype(F32).T
        low = (rows % LO).astype(F32)
        lo_ref[...] = low.T if nt else low

    sub = lax.broadcasted_iota(jnp.int32, (requests, span), 0)
    lane = lax.broadcasted_iota(jnp.int32, (requests, span), 1)
    own = lane // bag == sub
    one = jnp.ones((), BF)
    zero = jnp.zeros((), BF)
    if nt:
        lo_iota = lax.broadcasted_iota(jnp.int32, (LO, span), 0).astype(F32).astype(BF)
    else:
        lo_iota = lax.broadcasted_iota(jnp.int32, (span, LO), 1).astype(F32).astype(BF)

    def one_owner(o):
        row = jnp.broadcast_to(hi_ref[pl.ds(o, 1), :], (requests, span))
        code = jnp.where(own, row, 4.0 * HI)
        pair = jnp.concatenate([code, code - 1.0], axis=0).astype(BF)
        lhs = jnp.concatenate([jnp.where(pair == BF(2 * k), one, zero) for k in range(HI // 2)], axis=0)
        if nt:
            col = jnp.broadcast_to(lo_ref[pl.ds(o, 1), :], (16, span)).astype(BF)
            col = jnp.concatenate([col] * (LO // 16), axis=0)
            rhs = jnp.where(col == lo_iota, one, zero)
            return lax.dot_general(lhs.astype(F8), rhs.astype(F8), (((1,), (1,)), ((), ())), preferred_element_type=F32)
        col = jnp.broadcast_to(lo_ref[:, o : o + 1].astype(BF), (span, LO))
        rhs = jnp.where(col == lo_iota, one, zero)
        return jnp.dot(lhs.astype(F8), rhs.astype(F8), preferred_element_type=F32)

    def build(q, tally_ref):
        quad = [one_owner(4 * q + u) for u in range(4)]
        at = q * 32
        for k in range(HI):
            rows_k = jnp.concatenate([a[k * 8 : k * 8 + 8] for a in quad], axis=0)
            tally_ref[at : at + 32, k * LO : (k + 1) * LO] = rows_k.astype(F8)

    def split(c, tab_ref):
        piece = slice(c * depth, (c + 1) * depth)
        scaled = table_ref[0, piece, :].astype(F32) * UP
        coarse = scaled.astype(F8)
        tab_ref[piece, :width0] = coarse
        tab_ref[piece, width0:] = ((scaled - coarse.astype(F32)) * FINE).astype(F8)

    width0 = table_ref.shape[2]
    quads = owners // 4
    depth = total_rows // chunks
    per = quads // chunks

    def gather(c, tally_ref, tab_ref):
        part = jnp.dot(
            tally_ref[:, c * depth : (c + 1) * depth],
            tab_ref[c * depth : (c + 1) * depth, :],
            preferred_element_type=F32,
        )
        if c == 0:
            acc_ref[...] = part
        else:
            acc_ref[...] += part

    def finish():
        pooled = ((acc_ref[:, :width0] + acc_ref[:, width0:] * (1.0 / FINE)) * (1.0 / UP)).astype(BF)
        part = jnp.dot(pooled, proj_ref[0], preferred_element_type=F32)
        total_ref[...] = jnp.where(step == 1, part, total_ref[...] + part)

    @pl.when(step == 0)
    def _():
        small_ref[...] = jnp.zeros_like(small_ref)
        h2, h3 = b2_ref.shape[1], b3_ref.shape[1]
        small_ref[0:1, :] = b1_ref[...]
        small_ref[1:2, :h2] = b2_ref[...]
        small_ref[1:2, h2 : h2 + h3] = b3_ref[...]
        small_ref[1:2, h2 + h3 :] = ws_ref[...].astype(F32)
        small_ref[2:5, : cb_ref.shape[1]] = cb_ref[...]
        prepare()
        for c in range(chunks):
            split(c, tab_a)
            for q in range(c * per, (c + 1) * per):
                build(q, tally_a)

    for parity, new, old in ((0, (tally_a, tab_a), (tally_b, tab_b)), (1, (tally_b, tab_b), (tally_a, tab_a))):

        @pl.when((step > 0) & (step < last) & (lax.rem(step, 2) == parity))
        def _(new=new, old=old):
            prepare()
            for c in range(chunks):
                gather(c, *old)
                split(c, new[1])
                for q in range(c * per, (c + 1) * per):
                    build(q, new[0])
            finish()

    @pl.when(step == last)
    def _():
        for c in range(chunks):
            gather(c, tally_b, tab_b)
        finish()
        core = lax.rem(lax.axis_index(axis), 2)
        for q in range(owners // 2):
            to = slice(q * requests, (q + 1) * requests)
            mine_ref[to, :] = total_ref[pl.ds(pl.multiple_of((2 * q + core) * requests, requests), requests), :]
        for q in range(0, owners // 2, 2):
            two = [
                total_ref[pl.ds(pl.multiple_of((2 * p + 1 - core) * requests, requests), requests), :] for p in (q, q + 1)
            ]
            twin_ref[q * requests : (q + 2) * requests, :] = jnp.concatenate(two, axis=0).astype(BF)


def pool(tables, projections, bag_rows, bag_lengths, b1, b2, b3, cb, ws, axis="table", chunks=16, nt=True):
    ntab, rows, e = tables.shape
    owners, requests, bag = bag_rows.shape[1], bag_rows.shape[3], bag_rows.shape[4]
    width = projections.shape[2]
    r = bag_rows.transpose(0, 2, 3, 4, 1).reshape(ntab, requests * bag, owners)
    l = bag_lengths.transpose(0, 2, 3, 1).reshape(ntab, requests, owners)
    bags = owners * requests
    span = requests * bag
    ahead = lambda i: (jnp.minimum(i, ntab - 1), 0, 0)
    behind = lambda i: (jnp.maximum(i - 1, 0), 0, 0)
    rest = (b1[None], b2[None], b3[None], cb, ws[None])
    fixed = lambda shape: pl.BlockSpec(shape, lambda i: (0, 0))
    return pl.pallas_call(
        functools.partial(pool_kernel, chunks=chunks, nt=nt, axis=axis),
        grid=(ntab + 1,),
        in_specs=[
            pl.BlockSpec((1, span, owners), ahead),
            pl.BlockSpec((1, requests, owners), ahead),
            pl.BlockSpec((1, rows, e), ahead),
            pl.BlockSpec((1, e, width), behind),
        ] + [fixed(a.shape) for a in rest],
        out_specs=[fixed((bags // 2, width)), fixed((bags // 2, width)), fixed((8, b1.shape[0]))],
        out_shape=[
            jax.ShapeDtypeStruct((bags // 2, width), F32),
            jax.ShapeDtypeStruct((bags // 2, width), BF),
            jax.ShapeDtypeStruct((8, b1.shape[0]), F32),
        ],
        scratch_shapes=[
            pltpu.VMEM((owners, span), F32),
            pltpu.VMEM((owners, span) if nt else (span, owners), F32),
            pltpu.VMEM((bags, rows), F8),
            pltpu.VMEM((bags, rows), F8),
            pltpu.VMEM((rows, 2 * e), F8),
            pltpu.VMEM((rows, 2 * e), F8),
            pltpu.VMEM((bags, 2 * e), F32),
            pltpu.VMEM((bags, width), F32),
        ],
        compiler_params=pltpu.CompilerParams(vmem_limit_bytes=56 << 20),
        name="pool",
    )(r, l, tables, projections, *rest)


def score_kernel(counts_ref, got_ref, feat_ref, down_ref, up_ref, w1, w2, w3, small_ref, out_ref, ctx_ref, *, sub):
    step = pl.program_id(0)
    block = feat_ref.shape[0]
    requests = counts_ref.shape[0]
    width = up_ref.shape[2]

    @pl.when(step == 0)
    def _():
        got = got_ref[...].astype(F32)
        ctx_ref[...] = jnp.sum(got.reshape(-1, requests, got.shape[1]), axis=0).astype(BF)

    h2, h3 = w2.shape[1], w3.shape[1]
    b1, b2, b3 = small_ref[0:1, :], small_ref[1:2, :h2], small_ref[1:2, h2 : h2 + h3]
    ws = small_ref[1:2, h2 + h3 :].astype(BF)
    ends = []
    total = jnp.int32(0)
    for r in range(requests):
        total = total + counts_ref[r]
        ends.append(total)
    base = step * block

    @pl.when(base >= total)
    def _():
        out_ref[...] = jnp.zeros_like(out_ref)

    @pl.when(base < total)
    def _():
        lane = lax.broadcasted_iota(jnp.int32, (1, requests), 1)
        end_row = jnp.zeros((1, requests), jnp.int32)
        start_row = jnp.zeros((1, requests), jnp.int32)
        for r in range(requests):
            end_row = jnp.where(lane == r, ends[r], end_row)
            if r:
                start_row = jnp.where(lane == r, ends[r - 1], start_row)
        xs, anchors = [], []
        n = block // sub
        for i in range(n):
            pos = base + i * sub + lax.broadcasted_iota(jnp.int32, (sub, requests), 0)
            choose = ((pos >= start_row) & (pos < end_row)).astype(F32).astype(BF)
            rows = jnp.dot(choose, ctx_ref[...], preferred_element_type=F32)
            a = jnp.concatenate([feat_ref[i * sub : (i + 1) * sub, :].astype(F32), rows], axis=1)
            anchors.append(a)
            xs.append(a)
        for l in range(down_ref.shape[0]):
            red = [jnp.dot(x.astype(BF), down_ref[l], preferred_element_type=F32).astype(BF) for x in xs]
            xs = [
                a * (jnp.dot(r, up_ref[l], preferred_element_type=F32) + small_ref[2 + l : 3 + l, :width]) + x
                for a, r, x in zip(anchors, red, xs)
            ]
        hs = [x.astype(BF) for x in xs]
        for w, b in ((w1, b1), (w2, b2), (w3, b3)):
            hs = [jnp.maximum(jnp.dot(h, w[...], preferred_element_type=F32) + b, 0.0).astype(BF) for h in hs]
        for i, h in enumerate(hs):
            s = lax.dot_general(ws, h, (((1,), (1,)), ((), ())), preferred_element_type=F32)
            at = base + i * sub + lax.broadcasted_iota(jnp.int32, (1, sub), 1)
            out_ref[:, i * sub : (i + 1) * sub] = jnp.where(at < total, s, 0.0)


def score(got, counts, features, cross_down, cross_up, w1, w2, w3, small, block=1024, sub=512):
    slots, width = features.shape
    requests = counts.shape[0]
    whole = lambda a: pl.BlockSpec(a.shape, lambda i, c: (0,) * a.ndim)
    rest = (cross_down, cross_up, w1, w2, w3, small)
    return pl.pallas_call(
        functools.partial(score_kernel, sub=sub),
        grid_spec=pltpu.PrefetchScalarGridSpec(
            num_scalar_prefetch=1,
            grid=(slots // block,),
            in_specs=[whole(got), pl.BlockSpec((block, width), lambda i, c: (i, 0))] + [whole(a) for a in rest],
            out_specs=pl.BlockSpec((1, block), lambda i, c: (0, i)),
            scratch_shapes=[pltpu.VMEM((requests, width), BF)],
        ),
        out_shape=jax.ShapeDtypeStruct((1, slots), F32),
        compiler_params=pltpu.CompilerParams(vmem_limit_bytes=40 << 20),
        name="score",
    )(counts, got, features, *rest)


def body(
    tables, projections, bag_rows, bag_lengths, candidates, request_counts,
    cross_down, cross_up, cross_bias, w1, b1, w2, b2, w3, b3, ws,
):
    owners, requests, width = bag_rows.shape[1], bag_rows.shape[3], projections.shape[2]
    mine, twin, small = pool(tables, projections, bag_rows, bag_lengths, b1, b2, b3, cross_bias, ws)
    other = lax.ppermute(twin, "table", [(t, t ^ 1) for t in range(owners)])
    sums = (mine + other.astype(F32)).astype(BF).reshape(owners // 2, requests, width)
    groups = [list(range(c, owners, 2)) for c in range(2)]
    got = lax.all_to_all(sums, "table", split_axis=0, concat_axis=0, axis_index_groups=groups, tiled=True)
    got = got.reshape(owners // 2 * requests, width)
    return score(got, request_counts[0, 0], candidates[0, 0], cross_down, cross_up, w1, w2, w3, small)[None]


def solution(mesh):
    in_specs = (
        P("table", None, None),
        P("table", None, None),
        P("table", None, "helper", None, None),
        P("table", None, "helper", None),
        P("table", "helper", None, None),
        P("table", "helper", None),
    ) + (P(),) * 10
    out_specs = P("table", "helper", None)
    return jax.shard_map(body, mesh=mesh, in_specs=in_specs, out_specs=out_specs, check_vma=False)
```

```python
import functools

import jax
import jax.numpy as jnp
from jax import lax
from jax.experimental import pallas as pl
from jax.experimental.pallas import tpu as pltpu
from jax.sharding import PartitionSpec as P

F32 = jnp.float32
BF = jnp.bfloat16
HI = 16
LO = 256
F8 = jnp.float8_e4m3fn
UP = 64.0
FINE = 16.0


def pool_kernel(
    rows_ref, lens_ref, table_ref, proj_ref, b1_ref, b2_ref, b3_ref, cb_ref, ws_ref,
    mine_ref, twin_ref, small_ref, hi_ref, lo_ref, tally_a, tally_b, tab_a, tab_b, acc_ref, total_ref, *, chunks, nt, axis
):
    step = pl.program_id(0)
    last = pl.num_programs(0) - 1
    owners = rows_ref.shape[2]
    span = rows_ref.shape[1]
    requests = lens_ref.shape[1]
    bag = span // requests
    total_rows = table_ref.shape[1]

    def prepare():
        rows = rows_ref[0]
        place = lax.broadcasted_iota(jnp.int32, (requests, bag, owners), 1)
        used = (place < lens_ref[0][:, None, :]).reshape(span, owners)
        hi_ref[...] = jnp.where(used, rows // LO, 4 * HI).astype(F32).T
        low = (rows % LO).astype(F32)
        lo_ref[...] = low.T if nt else low

    sub = lax.broadcasted_iota(jnp.int32, (requests, span), 0)
    lane = lax.broadcasted_iota(jnp.int32, (requests, span), 1)
    own = lane // bag == sub
    one = jnp.ones((), BF)
    zero = jnp.zeros((), BF)
    if nt:
        lo_iota = lax.broadcasted_iota(jnp.int32, (LO, span), 0).astype(F32).astype(BF)
    else:
        lo_iota = lax.broadcasted_iota(jnp.int32, (span, LO), 1).astype(F32).astype(BF)

    def one_owner(o):
        row = jnp.broadcast_to(hi_ref[pl.ds(o, 1), :], (requests, span))
        code = jnp.where(own, row, 4.0 * HI)
        pair = jnp.concatenate([code, code - 1.0], axis=0).astype(BF)
        lhs = jnp.concatenate([jnp.where(pair == BF(2 * k), one, zero) for k in range(HI // 2)], axis=0)
        if nt:
            col = jnp.broadcast_to(lo_ref[pl.ds(o, 1), :], (16, span)).astype(BF)
            col = jnp.concatenate([col] * (LO // 16), axis=0)
            rhs = jnp.where(col == lo_iota, one, zero)
            return lax.dot_general(lhs.astype(F8), rhs.astype(F8), (((1,), (1,)), ((), ())), preferred_element_type=F32)
        col = jnp.broadcast_to(lo_ref[:, o : o + 1].astype(BF), (span, LO))
        rhs = jnp.where(col == lo_iota, one, zero)
        return jnp.dot(lhs.astype(F8), rhs.astype(F8), preferred_element_type=F32)

    def build(q, tally_ref):
        quad = [one_owner(4 * q + u) for u in range(4)]
        at = q * 32
        for k in range(HI):
            rows_k = jnp.concatenate([a[k * 8 : k * 8 + 8] for a in quad], axis=0)
            tally_ref[at : at + 32, k * LO : (k + 1) * LO] = rows_k.astype(F8)

    def split(c, tab_ref):
        piece = slice(c * depth, (c + 1) * depth)
        scaled = table_ref[0, piece, :].astype(F32) * UP
        coarse = scaled.astype(F8)
        tab_ref[piece, :width0] = coarse
        tab_ref[piece, width0:] = ((scaled - coarse.astype(F32)) * FINE).astype(F8)

    width0 = table_ref.shape[2]
    quads = owners // 4
    depth = total_rows // chunks
    per = quads // chunks

    def gather(c, tally_ref, tab_ref):
        part = jnp.dot(
            tally_ref[:, c * depth : (c + 1) * depth],
            tab_ref[c * depth : (c + 1) * depth, :],
            preferred_element_type=F32,
        )
        if c == 0:
            acc_ref[...] = part
        else:
            acc_ref[...] += part

    def finish():
        pooled = ((acc_ref[:, :width0] + acc_ref[:, width0:] * (1.0 / FINE)) * (1.0 / UP)).astype(BF)
        part = jnp.dot(pooled, proj_ref[0], preferred_element_type=F32)
        total_ref[...] = jnp.where(step == 1, part, total_ref[...] + part)

    @pl.when(step == 0)
    def _():
        small_ref[...] = jnp.zeros_like(small_ref)
        h2, h3 = b2_ref.shape[1], b3_ref.shape[1]
        small_ref[0:1, :] = b1_ref[...]
        small_ref[1:2, :h2] = b2_ref[...]
        small_ref[1:2, h2 : h2 + h3] = b3_ref[...]
        small_ref[1:2, h2 + h3 :] = ws_ref[...].astype(F32)[None]
        small_ref[2:5, : cb_ref.shape[1]] = cb_ref[...]
        prepare()
        for c in range(chunks):
            split(c, tab_a)
            for q in range(c * per, (c + 1) * per):
                build(q, tally_a)

    for parity, new, old in ((0, (tally_a, tab_a), (tally_b, tab_b)), (1, (tally_b, tab_b), (tally_a, tab_a))):

        @pl.when((step > 0) & (step < last) & (lax.rem(step, 2) == parity))
        def _(new=new, old=old):
            prepare()
            for c in range(chunks):
                gather(c, *old)
                split(c, new[1])
                for q in range(c * per, (c + 1) * per):
                    build(q, new[0])
            finish()

    @pl.when(step == last)
    def _():
        for c in range(chunks):
            gather(c, tally_b, tab_b)
        finish()
        core = lax.rem(lax.axis_index(axis), 2)
        for q in range(owners // 2):
            to = slice(q * requests, (q + 1) * requests)
            mine_ref[to, :] = total_ref[pl.ds(pl.multiple_of((2 * q + core) * requests, requests), requests), :]
        for q in range(0, owners // 2, 2):
            two = [
                total_ref[pl.ds(pl.multiple_of((2 * p + 1 - core) * requests, requests), requests), :] for p in (q, q + 1)
            ]
            twin_ref[q * requests : (q + 2) * requests, :] = jnp.concatenate(two, axis=0).astype(BF)


def pool(tables, projections, bag_rows, bag_lengths, b1, b2, b3, cb, ws, axis="table", chunks=16, nt=True):
    ntab, rows, e = tables.shape
    owners, requests, bag = bag_rows.shape[1], bag_rows.shape[3], bag_rows.shape[4]
    width = projections.shape[2]
    r = bag_rows.transpose(0, 2, 3, 4, 1).reshape(ntab, requests * bag, owners)
    l = bag_lengths.transpose(0, 2, 3, 1).reshape(ntab, requests, owners)
    bags = owners * requests
    span = requests * bag
    ahead = lambda i: (jnp.minimum(i, ntab - 1), 0, 0)
    behind = lambda i: (jnp.maximum(i - 1, 0), 0, 0)
    rest = (b1[None], b2[None], b3[None], cb, ws)
    fixed = lambda shape: pl.BlockSpec(shape, lambda i: (0,) * len(shape))
    return pl.pallas_call(
        functools.partial(pool_kernel, chunks=chunks, nt=nt, axis=axis),
        grid=(ntab + 1,),
        in_specs=[
            pl.BlockSpec((1, span, owners), ahead),
            pl.BlockSpec((1, requests, owners), ahead),
            pl.BlockSpec((1, rows, e), ahead),
            pl.BlockSpec((1, e, width), behind),
        ] + [fixed(a.shape) for a in rest],
        out_specs=[fixed((bags // 2, width)), fixed((bags // 2, width)), fixed((8, b1.shape[0]))],
        out_shape=[
            jax.ShapeDtypeStruct((bags // 2, width), F32),
            jax.ShapeDtypeStruct((bags // 2, width), BF),
            jax.ShapeDtypeStruct((8, b1.shape[0]), F32),
        ],
        scratch_shapes=[
            pltpu.VMEM((owners, span), F32),
            pltpu.VMEM((owners, span) if nt else (span, owners), F32),
            pltpu.VMEM((bags, rows), F8),
            pltpu.VMEM((bags, rows), F8),
            pltpu.VMEM((rows, 2 * e), F8),
            pltpu.VMEM((rows, 2 * e), F8),
            pltpu.VMEM((bags, 2 * e), F32),
            pltpu.VMEM((bags, width), F32),
        ],
        compiler_params=pltpu.CompilerParams(vmem_limit_bytes=24 << 20),
        name="pool",
    )(*(pltpu.with_memory_space_constraint(a, pltpu.HBM) for a in (r, l, tables, projections) + rest))


def score_kernel(counts_ref, got_ref, feat_ref, down_ref, up_ref, w1, w2, w3, small_ref, out_ref, ctx_ref, *, sub):
    step = pl.program_id(0)
    block = feat_ref.shape[0]
    requests = counts_ref.shape[0]
    width = up_ref.shape[2]

    @pl.when(step == 0)
    def _():
        got = got_ref[...].astype(F32)
        ctx_ref[...] = jnp.sum(got.reshape(-1, requests, got.shape[1]), axis=0).astype(BF)

    h2, h3 = w2.shape[1], w3.shape[1]
    b1, b2, b3 = small_ref[0:1, :], small_ref[1:2, :h2], small_ref[1:2, h2 : h2 + h3]
    ws = small_ref[1:2, h2 + h3 :].astype(BF)
    ends = []
    total = jnp.int32(0)
    for r in range(requests):
        total = total + counts_ref[r]
        ends.append(total)
    base = step * block

    @pl.when(base >= total)
    def _():
        out_ref[...] = jnp.zeros_like(out_ref)

    @pl.when(base < total)
    def _():
        lane = lax.broadcasted_iota(jnp.int32, (1, requests), 1)
        end_row = jnp.zeros((1, requests), jnp.int32)
        start_row = jnp.zeros((1, requests), jnp.int32)
        for r in range(requests):
            end_row = jnp.where(lane == r, ends[r], end_row)
            if r:
                start_row = jnp.where(lane == r, ends[r - 1], start_row)
        xs, anchors = [], []
        n = block // sub
        for i in range(n):
            pos = base + i * sub + lax.broadcasted_iota(jnp.int32, (sub, requests), 0)
            choose = ((pos >= start_row) & (pos < end_row)).astype(F32).astype(BF)
            rows = jnp.dot(choose, ctx_ref[...], preferred_element_type=F32)
            a = jnp.concatenate([feat_ref[i * sub : (i + 1) * sub, :].astype(F32), rows], axis=1)
            anchors.append(a)
            xs.append(a)
        for l in range(down_ref.shape[0]):
            red = [jnp.dot(x.astype(BF), down_ref[l], preferred_element_type=F32).astype(BF) for x in xs]
            xs = [
                a * (jnp.dot(r, up_ref[l], preferred_element_type=F32) + small_ref[2 + l : 3 + l, :width]) + x
                for a, r, x in zip(anchors, red, xs)
            ]
        hs = [x.astype(BF) for x in xs]
        for w, b in ((w1, b1), (w2, b2), (w3, b3)):
            hs = [jnp.maximum(jnp.dot(h, w[...], preferred_element_type=F32) + b, 0.0).astype(BF) for h in hs]
        for i, h in enumerate(hs):
            s = lax.dot_general(ws, h, (((1,), (1,)), ((), ())), preferred_element_type=F32)
            at = base + i * sub + lax.broadcasted_iota(jnp.int32, (1, sub), 1)
            out_ref[:, i * sub : (i + 1) * sub] = jnp.where(at < total, s, 0.0)


def score(got, counts, features, cross_down, cross_up, w1, w2, w3, small, block=2048, sub=512):
    slots, width = features.shape
    requests = counts.shape[0]
    whole = lambda a: pl.BlockSpec(a.shape, lambda i, c: (0,) * a.ndim)
    rest = (cross_down, cross_up, w1, w2, w3, small)
    return pl.pallas_call(
        functools.partial(score_kernel, sub=sub),
        grid_spec=pltpu.PrefetchScalarGridSpec(
            num_scalar_prefetch=1,
            grid=(slots // block,),
            in_specs=[whole(got), pl.BlockSpec((block, width), lambda i, c: (i, 0))] + [whole(a) for a in rest],
            out_specs=pl.BlockSpec((1, block), lambda i, c: (0, i)),
            scratch_shapes=[pltpu.VMEM((requests, width), BF)],
        ),
        out_shape=jax.ShapeDtypeStruct((1, slots), F32),
        compiler_params=pltpu.CompilerParams(vmem_limit_bytes=40 << 20),
        name="score",
    )(counts, got, features, *rest)


def body(
    tables, projections, bag_rows, bag_lengths, candidates, request_counts,
    cross_down, cross_up, cross_bias, w1, b1, w2, b2, w3, b3, ws,
):
    owners, requests, width = bag_rows.shape[1], bag_rows.shape[3], projections.shape[2]
    mine, twin, small = pool(tables, projections, bag_rows, bag_lengths, b1, b2, b3, cross_bias, ws)
    other = lax.ppermute(twin, "table", [(t, t ^ 1) for t in range(owners)])
    sums = (mine + other.astype(F32)).astype(BF).reshape(owners // 2, requests, width)
    groups = [list(range(c, owners, 2)) for c in range(2)]
    got = lax.all_to_all(sums, "table", split_axis=0, concat_axis=0, axis_index_groups=groups, tiled=True)
    got = got.reshape(owners // 2 * requests, width)
    return score(got, request_counts[0, 0], candidates[0, 0], cross_down, cross_up, w1, w2, w3, small)[None]


def solution(mesh):
    in_specs = (
        P("table", None, None),
        P("table", None, None),
        P("table", None, "helper", None, None),
        P("table", None, "helper", None),
        P("table", "helper", None, None),
        P("table", "helper", None),
    ) + (P(),) * 10
    out_specs = P("table", "helper", None)
    return jax.shard_map(body, mesh=mesh, in_specs=in_specs, out_specs=out_specs, check_vma=False)
```

```python
import functools

import jax
import jax.numpy as jnp
from jax import lax
from jax.experimental import pallas as pl
from jax.experimental.pallas import tpu as pltpu
from jax.sharding import PartitionSpec as P

F32 = jnp.float32
BF = jnp.bfloat16
HI = 16
LO = 256
F8 = jnp.float8_e4m3fn
UP = 64.0
FINE = 16.0


def pool_kernel(
    rows_ref, lens_ref, table_ref, proj_ref, b1_ref, b2_ref, b3_ref, cb_ref, ws_ref,
    mine_ref, twin_ref, small_ref, hi_ref, lo_ref, tally_a, tally_b, tab_a, tab_b, acc_ref, total_ref, *, chunks, axis
):
    step = pl.program_id(0)
    last = pl.num_programs(0) - 1
    owners = rows_ref.shape[2]
    span = rows_ref.shape[1]
    requests = lens_ref.shape[1]
    bag = span // requests
    total_rows = table_ref.shape[1]

    def prepare():
        rows = rows_ref[0]
        place = lax.broadcasted_iota(jnp.int32, (requests, bag, owners), 1)
        used = (place < lens_ref[0][:, None, :]).reshape(span, owners)
        hi_ref[...] = jnp.where(used, rows // LO, 4 * HI).astype(F32).T
        lo_ref[...] = (rows % LO - LO // 2).astype(F32).T

    sub = lax.broadcasted_iota(jnp.int32, (requests, span), 0)
    lane = lax.broadcasted_iota(jnp.int32, (requests, span), 1)
    own = lane // bag == sub
    low_all = (lax.broadcasted_iota(jnp.int32, (LO, span), 0) - LO // 2).astype(jnp.int8)
    one = jnp.ones((32, span), F8)
    zero = jnp.zeros((32, span), F8)

    def one_owner(o):
        row = jnp.broadcast_to(hi_ref[o : o + 1, :], (requests, span))
        code = jnp.where(own, row, 4.0 * HI)
        four = jnp.concatenate([code, code - 1.0, code - 2.0, code - 3.0], axis=0).astype(jnp.int32).astype(jnp.int8)
        lhs = jnp.concatenate(
            [jnp.where(four == jnp.full((32, span), 4 * k, jnp.int8), one, zero) for k in range(HI // 4)], axis=0
        )
        low = jnp.broadcast_to(lo_ref[o : o + 1, :], (32, span)).astype(jnp.int32).astype(jnp.int8)
        rhs = jnp.concatenate(
            [jnp.where(low == low_all[32 * v : 32 * v + 32], one, zero) for v in range(LO // 32)], axis=0
        )
        return lax.dot_general(lhs, rhs, (((1,), (1,)), ((), ())), preferred_element_type=F32)

    def build(q, tally_ref):
        quad = [one_owner(4 * q + u) for u in range(4)]
        at = q * 32
        for k in range(HI):
            rows_k = jnp.concatenate([a[k * 8 : k * 8 + 8] for a in quad], axis=0)
            tally_ref[at : at + 32, k * LO : (k + 1) * LO] = rows_k.astype(F8)

    def split(c, tab_ref):
        piece = slice(c * depth, (c + 1) * depth)
        scaled = table_ref[0, piece, :].astype(F32) * UP
        coarse = scaled.astype(F8)
        tab_ref[piece, :width0] = coarse
        tab_ref[piece, width0:] = ((scaled - coarse.astype(F32)) * FINE).astype(F8)

    width0 = table_ref.shape[2]
    quads = owners // 4
    depth = total_rows // chunks
    per = quads // chunks

    def gather(c, tally_ref, tab_ref):
        part = jnp.dot(
            tally_ref[:, c * depth : (c + 1) * depth],
            tab_ref[c * depth : (c + 1) * depth, :],
            preferred_element_type=F32,
        )
        if c == 0:
            acc_ref[...] = part
        else:
            acc_ref[...] += part

    def finish():
        pooled = ((acc_ref[:, :width0] + acc_ref[:, width0:] * (1.0 / FINE)) * (1.0 / UP)).astype(BF)
        part = jnp.dot(pooled, proj_ref[0], preferred_element_type=F32)
        total_ref[...] = jnp.where(step == 1, part, total_ref[...] + part)

    @pl.when(step == 0)
    def _():
        small_ref[...] = jnp.zeros_like(small_ref)
        h2, h3 = b2_ref.shape[1], b3_ref.shape[1]
        small_ref[0:1, :] = b1_ref[...]
        small_ref[1:2, :h2] = b2_ref[...]
        small_ref[1:2, h2 : h2 + h3] = b3_ref[...]
        small_ref[1:2, h2 + h3 :] = ws_ref[...].astype(F32)[None]
        small_ref[2:5, : cb_ref.shape[1]] = cb_ref[...]
        prepare()
        for c in range(chunks):
            split(c, tab_a)
            for q in range(c * per, (c + 1) * per):
                build(q, tally_a)

    for parity, new, old in ((0, (tally_a, tab_a), (tally_b, tab_b)), (1, (tally_b, tab_b), (tally_a, tab_a))):

        @pl.when((step > 0) & (step < last) & (lax.rem(step, 2) == parity))
        def _(new=new, old=old):
            prepare()
            for c in range(chunks):
                gather(c, *old)
                split(c, new[1])
                for q in range(c * per, (c + 1) * per):
                    build(q, new[0])
            finish()

    @pl.when(step == last)
    def _():
        for c in range(chunks):
            gather(c, tally_b, tab_b)
        finish()
        core = lax.rem(lax.axis_index(axis), 2)
        for q in range(owners // 2):
            to = slice(q * requests, (q + 1) * requests)
            mine_ref[to, :] = total_ref[pl.ds(pl.multiple_of((2 * q + core) * requests, requests), requests), :]
        for q in range(0, owners // 2, 2):
            two = [
                total_ref[pl.ds(pl.multiple_of((2 * p + 1 - core) * requests, requests), requests), :] for p in (q, q + 1)
            ]
            twin_ref[q * requests : (q + 2) * requests, :] = jnp.concatenate(two, axis=0).astype(BF)


def pool(tables, projections, bag_rows, bag_lengths, b1, b2, b3, cb, ws, axis="table", chunks=16):
    ntab, rows, e = tables.shape
    owners, requests, bag = bag_rows.shape[1], bag_rows.shape[3], bag_rows.shape[4]
    width = projections.shape[2]
    r = bag_rows.transpose(0, 2, 3, 4, 1).reshape(ntab, requests * bag, owners)
    l = bag_lengths.transpose(0, 2, 3, 1).reshape(ntab, requests, owners)
    bags = owners * requests
    span = requests * bag
    ahead = lambda i: (jnp.minimum(i, ntab - 1), 0, 0)
    behind = lambda i: (jnp.maximum(i - 1, 0), 0, 0)
    rest = (b1[None], b2[None], b3[None], cb, ws)
    fixed = lambda shape: pl.BlockSpec(shape, lambda i: (0,) * len(shape))
    return pl.pallas_call(
        functools.partial(pool_kernel, chunks=chunks, axis=axis),
        grid=(ntab + 1,),
        in_specs=[
            pl.BlockSpec((1, span, owners), ahead),
            pl.BlockSpec((1, requests, owners), ahead),
            pl.BlockSpec((1, rows, e), ahead),
            pl.BlockSpec((1, e, width), behind),
        ] + [fixed(a.shape) for a in rest],
        out_specs=[fixed((bags // 2, width)), fixed((bags // 2, width)), fixed((8, b1.shape[0]))],
        out_shape=[
            jax.ShapeDtypeStruct((bags // 2, width), F32),
            jax.ShapeDtypeStruct((bags // 2, width), BF),
            jax.ShapeDtypeStruct((8, b1.shape[0]), F32),
        ],
        scratch_shapes=[
            pltpu.VMEM((owners, span), F32),
            pltpu.VMEM((owners, span), F32),
            pltpu.VMEM((bags, rows), F8),
            pltpu.VMEM((bags, rows), F8),
            pltpu.VMEM((rows, 2 * e), F8),
            pltpu.VMEM((rows, 2 * e), F8),
            pltpu.VMEM((bags, 2 * e), F32),
            pltpu.VMEM((bags, width), F32),
        ],
        compiler_params=pltpu.CompilerParams(vmem_limit_bytes=24 << 20),
        name="pool",
    )(*(pltpu.with_memory_space_constraint(a, pltpu.HBM) for a in (r, l, tables, projections) + rest))


def score_kernel(counts_ref, got_ref, feat_ref, down_ref, up_ref, w1, w2, w3, small_ref, out_ref, *, sub):
    slots = feat_ref.shape[0]
    requests = counts_ref.shape[0]
    width = up_ref.shape[2]
    got = got_ref[...].astype(F32)
    context = jnp.sum(got.reshape(-1, requests, got.shape[1]), axis=0).astype(BF)
    h2, h3 = w2.shape[1], w3.shape[1]
    b1, b2, b3 = small_ref[0:1, :], small_ref[1:2, :h2], small_ref[1:2, h2 : h2 + h3]
    ws = small_ref[1:2, h2 + h3 :].astype(BF)
    ends = []
    total = jnp.int32(0)
    for r in range(requests):
        total = total + counts_ref[r]
        ends.append(total)
    lane = lax.broadcasted_iota(jnp.int32, (1, requests), 1)
    end_row = jnp.zeros((1, requests), jnp.int32)
    start_row = jnp.zeros((1, requests), jnp.int32)
    for r in range(requests):
        end_row = jnp.where(lane == r, ends[r], end_row)
        if r:
            start_row = jnp.where(lane == r, ends[r - 1], start_row)

    def run(parts):
        anchors = []
        for i in range(parts):
            pos = i * sub + lax.broadcasted_iota(jnp.int32, (sub, requests), 0)
            choose = ((pos >= start_row) & (pos < end_row)).astype(F32).astype(BF)
            rows = jnp.dot(choose, context, preferred_element_type=F32)
            anchors.append(jnp.concatenate([feat_ref[i * sub : (i + 1) * sub, :].astype(F32), rows], axis=1))
        xs = anchors
        for l in range(down_ref.shape[0]):
            red = [jnp.dot(x.astype(BF), down_ref[l], preferred_element_type=F32).astype(BF) for x in xs]
            xs = [
                a * (jnp.dot(r, up_ref[l], preferred_element_type=F32) + small_ref[2 + l : 3 + l, :width]) + x
                for a, r, x in zip(anchors, red, xs)
            ]
        hs = [x.astype(BF) for x in xs]
        for w, b in ((w1, b1), (w2, b2), (w3, b3)):
            hs = [jnp.maximum(jnp.dot(h, w[...], preferred_element_type=F32) + b, 0.0).astype(BF) for h in hs]
        for i, h in enumerate(hs):
            s = lax.dot_general(ws, h, (((1,), (1,)), ((), ())), preferred_element_type=F32)
            at = i * sub + lax.broadcasted_iota(jnp.int32, (1, sub), 1)
            out_ref[:, i * sub : (i + 1) * sub] = jnp.where(at < total, s, 0.0)
        if parts * sub < slots:
            out_ref[:, parts * sub :] = jnp.zeros((1, slots - parts * sub), F32)

    half = slots // sub // 2

    @pl.when(total > half * sub)
    def _():
        run(slots // sub)

    @pl.when(total <= half * sub)
    def _():
        run(half)


def score(got, counts, features, cross_down, cross_up, w1, w2, w3, small, block=2048, sub=512):
    slots, width = features.shape
    whole = lambda a: pl.BlockSpec(a.shape, lambda i, c: (0,) * a.ndim)
    rest = (cross_down, cross_up, w1, w2, w3, small)
    return pl.pallas_call(
        functools.partial(score_kernel, sub=sub),
        grid_spec=pltpu.PrefetchScalarGridSpec(
            num_scalar_prefetch=1,
            grid=(slots // block,),
            in_specs=[whole(got), pl.BlockSpec((block, width), lambda i, c: (i, 0))] + [whole(a) for a in rest],
            out_specs=pl.BlockSpec((1, block), lambda i, c: (0, i)),
        ),
        out_shape=jax.ShapeDtypeStruct((1, slots), F32),
        compiler_params=pltpu.CompilerParams(vmem_limit_bytes=40 << 20),
        name="score",
    )(counts, got, features, *rest)


def body(
    tables, projections, bag_rows, bag_lengths, candidates, request_counts,
    cross_down, cross_up, cross_bias, w1, b1, w2, b2, w3, b3, ws,
):
    owners, requests, width = bag_rows.shape[1], bag_rows.shape[3], projections.shape[2]
    mine, twin, small = pool(tables, projections, bag_rows, bag_lengths, b1, b2, b3, cross_bias, ws)
    other = lax.ppermute(twin, "table", [(t, t ^ 1) for t in range(owners)])
    sums = (mine + other.astype(F32)).astype(BF).reshape(owners // 2, requests, width)
    groups = [list(range(c, owners, 2)) for c in range(2)]
    got = lax.all_to_all(sums, "table", split_axis=0, concat_axis=0, axis_index_groups=groups, tiled=True)
    got = got.reshape(owners // 2 * requests, width)
    return score(got, request_counts[0, 0], candidates[0, 0], cross_down, cross_up, w1, w2, w3, small)[None]


def solution(mesh):
    in_specs = (
        P("table", None, None),
        P("table", None, None),
        P("table", None, "helper", None, None),
        P("table", None, "helper", None),
        P("table", "helper", None, None),
        P("table", "helper", None),
    ) + (P(),) * 10
    out_specs = P("table", "helper", None)
    return jax.shard_map(body, mesh=mesh, in_specs=in_specs, out_specs=out_specs, check_vma=False)
```

```python
import functools

import jax
import jax.numpy as jnp
from jax import lax
from jax.experimental import pallas as pl
from jax.experimental.pallas import tpu as pltpu
from jax.sharding import PartitionSpec as P

F32 = jnp.float32
BF = jnp.bfloat16
HI = 16
LO = 256
F8 = jnp.float8_e4m3fn
UP = 64.0
FINE = 16.0


def pool_kernel(
    rows_ref, lens_ref, table_ref, proj_ref, b1_ref, b2_ref, b3_ref, cb_ref, ws_ref,
    mine_ref, twin_ref, small_ref, hi_ref, lo_ref, tally_a, tally_b, tab_a, tab_b, acc_ref, total_ref, *, chunks, axis
):
    step = pl.program_id(0)
    last = pl.num_programs(0) - 1
    owners = rows_ref.shape[2]
    span = rows_ref.shape[1]
    requests = lens_ref.shape[1]
    bag = span // requests
    total_rows = table_ref.shape[1]

    def prepare():
        rows = rows_ref[0]
        place = lax.broadcasted_iota(jnp.int32, (requests, bag, owners), 1)
        used = (place < lens_ref[0][:, None, :]).reshape(span, owners)
        hi_ref[...] = jnp.where(used, rows // LO, 4 * HI).astype(F32).T.astype(jnp.int32)
        lo_ref[...] = (rows % LO - LO // 2).astype(F32).T.astype(jnp.int32)

    sub = lax.broadcasted_iota(jnp.int32, (requests, span), 0)
    lane = lax.broadcasted_iota(jnp.int32, (requests, span), 1)
    own = lane // bag == sub
    low_all = (lax.broadcasted_iota(jnp.int32, (LO, span), 0) - LO // 2).astype(jnp.int8)
    one = jnp.ones((32, span), F8)
    zero = jnp.zeros((32, span), F8)

    def one_owner(o):
        row = jnp.broadcast_to(hi_ref[o : o + 1, :], (requests, span))
        code = jnp.where(own, row, 4 * HI)
        four = jnp.concatenate([code, code - 1, code - 2, code - 3], axis=0).astype(jnp.int8)
        lhs = jnp.concatenate(
            [jnp.where(four == jnp.full((32, span), 4 * k, jnp.int8), one, zero) for k in range(HI // 4)], axis=0
        )
        low = jnp.broadcast_to(lo_ref[o : o + 1, :], (32, span)).astype(jnp.int8)
        rhs = jnp.concatenate(
            [jnp.where(low == low_all[32 * v : 32 * v + 32], one, zero) for v in range(LO // 32)], axis=0
        )
        return lax.dot_general(lhs, rhs, (((1,), (1,)), ((), ())), preferred_element_type=F32)

    def build(q, tally_ref):
        quad = [one_owner(4 * q + u) for u in range(4)]
        at = q * 32
        for k in range(HI):
            rows_k = jnp.concatenate([a[k * 8 : k * 8 + 8] for a in quad], axis=0)
            tally_ref[at : at + 32, k * LO : (k + 1) * LO] = rows_k.astype(F8)

    def split(c, tab_ref):
        piece = slice(c * depth, (c + 1) * depth)
        scaled = table_ref[0, piece, :].astype(F32) * UP
        coarse = scaled.astype(F8)
        tab_ref[piece, :width0] = coarse
        tab_ref[piece, width0:] = ((scaled - coarse.astype(F32)) * FINE).astype(F8)

    width0 = table_ref.shape[2]
    quads = owners // 4
    depth = total_rows // chunks
    per = quads // chunks

    def gather(c, tally_ref, tab_ref):
        part = jnp.dot(
            tally_ref[:, c * depth : (c + 1) * depth],
            tab_ref[c * depth : (c + 1) * depth, :],
            preferred_element_type=F32,
        )
        if c == 0:
            acc_ref[...] = part
        else:
            acc_ref[...] += part

    def finish():
        pooled = ((acc_ref[:, :width0] + acc_ref[:, width0:] * (1.0 / FINE)) * (1.0 / UP)).astype(BF)
        part = jnp.dot(pooled, proj_ref[0], preferred_element_type=F32)
        total_ref[...] = jnp.where(step == 1, part, total_ref[...] + part)

    @pl.when(step == 0)
    def _():
        small_ref[...] = jnp.zeros_like(small_ref)
        h2, h3 = b2_ref.shape[1], b3_ref.shape[1]
        small_ref[0:1, :] = b1_ref[...]
        small_ref[1:2, :h2] = b2_ref[...]
        small_ref[1:2, h2 : h2 + h3] = b3_ref[...]
        small_ref[1:2, h2 + h3 :] = ws_ref[...].astype(F32)[None]
        small_ref[2:5, : cb_ref.shape[1]] = cb_ref[...]
        prepare()
        for c in range(chunks):
            split(c, tab_a)
            for q in range(c * per, (c + 1) * per):
                build(q, tally_a)

    for parity, new, old in ((0, (tally_a, tab_a), (tally_b, tab_b)), (1, (tally_b, tab_b), (tally_a, tab_a))):

        @pl.when((step > 0) & (step < last) & (lax.rem(step, 2) == parity))
        def _(new=new, old=old):
            prepare()
            for c in range(chunks):
                gather(c, *old)
                split(c, new[1])
                for q in range(c * per, (c + 1) * per):
                    build(q, new[0])
            finish()

    @pl.when(step == last)
    def _():
        for c in range(chunks):
            gather(c, tally_b, tab_b)
        finish()
        core = lax.rem(lax.axis_index(axis), 2)
        for q in range(owners // 2):
            to = slice(q * requests, (q + 1) * requests)
            mine_ref[to, :] = total_ref[pl.ds(pl.multiple_of((2 * q + core) * requests, requests), requests), :]
        for q in range(0, owners // 2, 2):
            two = [
                total_ref[pl.ds(pl.multiple_of((2 * p + 1 - core) * requests, requests), requests), :] for p in (q, q + 1)
            ]
            twin_ref[q * requests : (q + 2) * requests, :] = jnp.concatenate(two, axis=0).astype(BF)


def pool(tables, projections, bag_rows, bag_lengths, b1, b2, b3, cb, ws, axis="table", chunks=16):
    ntab, rows, e = tables.shape
    owners, requests, bag = bag_rows.shape[1], bag_rows.shape[3], bag_rows.shape[4]
    width = projections.shape[2]
    r = bag_rows.transpose(0, 2, 3, 4, 1).reshape(ntab, requests * bag, owners)
    l = bag_lengths.transpose(0, 2, 3, 1).reshape(ntab, requests, owners)
    bags = owners * requests
    span = requests * bag
    ahead = lambda i: (jnp.minimum(i, ntab - 1), 0, 0)
    behind = lambda i: (jnp.maximum(i - 1, 0), 0, 0)
    rest = (b1[None], b2[None], b3[None], cb, ws)
    fixed = lambda shape: pl.BlockSpec(shape, lambda i: (0,) * len(shape))
    return pl.pallas_call(
        functools.partial(pool_kernel, chunks=chunks, axis=axis),
        grid=(ntab + 1,),
        in_specs=[
            pl.BlockSpec((1, span, owners), ahead),
            pl.BlockSpec((1, requests, owners), ahead),
            pl.BlockSpec((1, rows, e), ahead),
            pl.BlockSpec((1, e, width), behind),
        ] + [fixed(a.shape) for a in rest],
        out_specs=[fixed((bags // 2, width)), fixed((bags // 2, width)), fixed((8, b1.shape[0]))],
        out_shape=[
            jax.ShapeDtypeStruct((bags // 2, width), F32),
            jax.ShapeDtypeStruct((bags // 2, width), BF),
            jax.ShapeDtypeStruct((8, b1.shape[0]), F32),
        ],
        scratch_shapes=[
            pltpu.VMEM((owners, span), jnp.int32),
            pltpu.VMEM((owners, span), jnp.int32),
            pltpu.VMEM((bags, rows), F8),
            pltpu.VMEM((bags, rows), F8),
            pltpu.VMEM((rows, 2 * e), F8),
            pltpu.VMEM((rows, 2 * e), F8),
            pltpu.VMEM((bags, 2 * e), F32),
            pltpu.VMEM((bags, width), F32),
        ],
        compiler_params=pltpu.CompilerParams(vmem_limit_bytes=24 << 20),
        name="pool",
    )(*(pltpu.with_memory_space_constraint(a, pltpu.HBM) for a in (r, l, tables, projections) + rest))


def score_kernel(counts_ref, got_ref, feat_ref, down_ref, up_ref, w1, w2, w3, small_ref, out_ref, *, sub):
    slots = feat_ref.shape[0]
    requests = counts_ref.shape[0]
    width = up_ref.shape[2]
    got = got_ref[...].astype(F32)
    context = jnp.sum(got.reshape(-1, requests, got.shape[1]), axis=0).astype(BF)
    h2, h3 = w2.shape[1], w3.shape[1]
    b1, b2, b3 = small_ref[0:1, :], small_ref[1:2, :h2], small_ref[1:2, h2 : h2 + h3]
    ws = small_ref[1:2, h2 + h3 :].astype(BF)
    ends = []
    total = jnp.int32(0)
    for r in range(requests):
        total = total + counts_ref[r]
        ends.append(total)
    lane = lax.broadcasted_iota(jnp.int32, (1, requests), 1)
    end_row = jnp.zeros((1, requests), jnp.int32)
    start_row = jnp.zeros((1, requests), jnp.int32)
    for r in range(requests):
        end_row = jnp.where(lane == r, ends[r], end_row)
        if r:
            start_row = jnp.where(lane == r, ends[r - 1], start_row)

    def run(parts):
        anchors = []
        for i in range(parts):
            pos = i * sub + lax.broadcasted_iota(jnp.int32, (sub, requests), 0)
            choose = ((pos >= start_row) & (pos < end_row)).astype(F32).astype(BF)
            rows = jnp.dot(choose, context, preferred_element_type=F32)
            anchors.append(jnp.concatenate([feat_ref[i * sub : (i + 1) * sub, :].astype(F32), rows], axis=1))
        layers, rank = down_ref.shape[0], down_ref.shape[2]
        xs = anchors
        red = [[] for _ in xs]
        shift = jnp.ones((1, width), F32)
        for l in range(layers):
            shift = shift + small_ref[2 + l : 3 + l, :width]
            for r, x in zip(red, xs):
                r.append(jnp.dot(x.astype(BF), down_ref[l], preferred_element_type=F32).astype(BF))
            if l < 2:
                up = up_ref[: l + 1].reshape((l + 1) * rank, width)
                ms = [jnp.dot(jnp.concatenate(r, axis=1), up, preferred_element_type=F32) + shift for r in red]
            else:
                ms = [m + (jnp.dot(r[l], up_ref[l], preferred_element_type=F32) + small_ref[2 + l : 3 + l, :width]) for m, r in zip(ms, red)]
            xs = [a * m for a, m in zip(anchors, ms)]
        hs = [x.astype(BF) for x in xs]
        for w, b in ((w1, b1), (w2, b2), (w3, b3)):
            hs = [jnp.maximum(jnp.dot(h, w[...], preferred_element_type=F32) + b, 0.0).astype(BF) for h in hs]
        for i, h in enumerate(hs):
            s = lax.dot_general(ws, h, (((1,), (1,)), ((), ())), preferred_element_type=F32)
            at = i * sub + lax.broadcasted_iota(jnp.int32, (1, sub), 1)
            out_ref[:, i * sub : (i + 1) * sub] = jnp.where(at < total, s, 0.0)
        if parts * sub < slots:
            out_ref[:, parts * sub :] = jnp.zeros((1, slots - parts * sub), F32)

    half = slots // sub // 2

    @pl.when(total > half * sub)
    def _():
        run(slots // sub)

    @pl.when(total <= half * sub)
    def _():
        run(half)


def score(got, counts, features, cross_down, cross_up, w1, w2, w3, small, block=2048, sub=512):
    slots, width = features.shape
    whole = lambda a: pl.BlockSpec(a.shape, lambda i, c: (0,) * a.ndim)
    rest = (cross_down, cross_up, w1, w2, w3, small)
    return pl.pallas_call(
        functools.partial(score_kernel, sub=sub),
        grid_spec=pltpu.PrefetchScalarGridSpec(
            num_scalar_prefetch=1,
            grid=(slots // block,),
            in_specs=[whole(got), pl.BlockSpec((block, width), lambda i, c: (i, 0))] + [whole(a) for a in rest],
            out_specs=pl.BlockSpec((1, block), lambda i, c: (0, i)),
        ),
        out_shape=jax.ShapeDtypeStruct((1, slots), F32),
        compiler_params=pltpu.CompilerParams(vmem_limit_bytes=40 << 20),
        name="score",
    )(counts, got, features, *rest)


def body(
    tables, projections, bag_rows, bag_lengths, candidates, request_counts,
    cross_down, cross_up, cross_bias, w1, b1, w2, b2, w3, b3, ws,
):
    owners, requests, width = bag_rows.shape[1], bag_rows.shape[3], projections.shape[2]
    mine, twin, small = pool(tables, projections, bag_rows, bag_lengths, b1, b2, b3, cross_bias, ws)
    other = lax.ppermute(twin, "table", [(t, t ^ 1) for t in range(owners)])
    sums = (mine + other.astype(F32)).astype(BF).reshape(owners // 2, requests, width)
    groups = [list(range(c, owners, 2)) for c in range(2)]
    got = lax.all_to_all(sums, "table", split_axis=0, concat_axis=0, axis_index_groups=groups, tiled=True)
    got = got.reshape(owners // 2 * requests, width)
    return score(got, request_counts[0, 0], candidates[0, 0], cross_down, cross_up, w1, w2, w3, small)[None]


def solution(mesh):
    in_specs = (
        P("table", None, None),
        P("table", None, None),
        P("table", None, "helper", None, None),
        P("table", None, "helper", None),
        P("table", "helper", None, None),
        P("table", "helper", None),
    ) + (P(),) * 10
    out_specs = P("table", "helper", None)
    return jax.shard_map(body, mesh=mesh, in_specs=in_specs, out_specs=out_specs, check_vma=False)
```
